512 devices in a mesh: seq: 32 (over z, core), mem: 16 (over y, x).
Axes of the slice: x: 4, y: 4, z: 16, core: 2. Of those that a mesh axis runs over, the one named last changes fastest.
Arguments:
- queries: bfloat16 [65536, 1024], P(('seq', 'mem'))
- local_keys: bfloat16 [65536, 1024], P(('seq', 'mem'))
- local_values: bfloat16 [65536, 1024], P(('seq', 'mem')), may hold values from -6 to 6
- memory_keys: bfloat16 [8192, 1024], P('mem')
- memory_values: bfloat16 [8192, 1024], P('mem'), may hold values from -6 to 6
- block_lists: int32 [1024, 8], P('seq'), may hold values from 0 to 127, as said below
- block_counts: int32 [1024], P('seq'), may hold values from 1 to 8
- doc_starts: int32 [4], replicated, may hold values from 0 to 65024, as said below
- gate_bias: float32 [8], replicated, may hold values from -2 to 2
Outputs:
- attended: bfloat16 [65536, 1024], P(('seq', 'mem'))
The draws below stay inside these ranges and needn't reach their ends.
Inputs may be any that keep to these rules, and one draw needn't show every extreme that they name: `block_lists`: slots at or past a query block's count are padding; a block may stand in several slots of one list. Query block i lists only blocks of shards o with o % 2 == (i + i // 2) % 2, and its slot 0 names a block of shard (i + i // 2) % 2; so of the 2 query blocks of one device, at most 1 lists blocks of a given shard (the other never does); for shard (i + i // 2) % 2 that block surely does, for other shards possibly none does. `doc_starts`: the first entry is 0; the entries do not fall (equal ones allowed); the last entry is 65024.
All inputs are finite; a program needn't handle non-finite values.
Results may differ from the reference program's by a relative error of at most 0.0105.
Values may be sent and summed in bfloat16 or wider, within the bound.
A program may use at most 64 MiB of HBM per device.

```python
import jax
import jax.numpy as jnp
from jax import lax

H = 8
HS = 128
HD = 1024
WINDOW = 1024
QBLK = 64
MBLK = 64
LIST = 8
DOCS = 4
QB_DEV = 2
TOKENS = 65536
NQB = 1024
MEM = 8192
NBLK = 128
BLK_DEV = 8
N_MEM = 16


def draw_queries(key, part):
    key = jax.random.fold_in(key, 1)
    key_base = jax.random.fold_in(key, 0)
    values = jax.random.normal(key_base, (TOKENS, HD), jnp.float32)
    return values.astype(jnp.bfloat16)


def draw_local_keys(key, part):
    key = jax.random.fold_in(key, 2)
    key_base = jax.random.fold_in(key, 0)
    values = jax.random.normal(key_base, (TOKENS, HD), jnp.float32)
    return values.astype(jnp.bfloat16)


def draw_memory_keys(key, part):
    key = jax.random.fold_in(key, 3)
    key_base = jax.random.fold_in(key, 0)
    values = jax.random.normal(key_base, (MEM, HD), jnp.float32)
    return values.astype(jnp.bfloat16)


def draw_block_lists(key, part):
    key = jax.random.fold_in(key, 5)
    key_first, key_second, key_within = jax.random.split(key, 3)
    block_ids = jnp.arange(NQB, dtype=jnp.int32)
    parity = (block_ids + block_ids // QB_DEV) % 2
    half_owners = N_MEM // 2
    first_pick = jax.random.randint(key_first, (NQB, LIST), 0, half_owners, dtype=jnp.int32)
    second_pick = jax.random.randint(key_second, (NQB, LIST), 0, half_owners, dtype=jnp.int32)
    owner_rank = jnp.minimum(first_pick, second_pick)
    slot_ids = jnp.arange(LIST, dtype=jnp.int32)
    owner_rank = jnp.where(slot_ids[None, :] == 0, 0, owner_rank)
    owner_ids = parity[:, None] + 2 * owner_rank
    within = jax.random.randint(key_within, (NQB, LIST), 0, BLK_DEV, dtype=jnp.int32)
    return (owner_ids * BLK_DEV + within).astype(jnp.int32)


def draw_doc_starts(key, part):
    key = jax.random.fold_in(key, 7)
    last_start = TOKENS - WINDOW // 2
    middle = jax.random.randint(key, (DOCS - 2,), 1, last_start, dtype=jnp.int32)
    return jnp.concatenate([jnp.zeros((1,), jnp.int32), jnp.sort(middle), jnp.full((1,), last_start, jnp.int32)]).astype(jnp.int32)


def touch_ends(values, rng, low, top_value):
    longest = values.shape.index(max(values.shape))
    spots = []
    for shift in (0, 1):
        where = [jax.random.randint(jax.random.fold_in(rng, axis), (), 0, length) for axis, length in enumerate(values.shape)]
        where[longest] = (where[longest] + shift) % values.shape[longest]
        spots.append(tuple(where))
    return values.at[spots[0]].set(low).at[spots[1]].set(top_value)


def level_of(own_key, dims, cuts, smallest, high):
    loudness = 1.0
    for position, shards_of in cuts:
        steps = jax.random.uniform(jax.random.fold_in(jax.random.fold_in(own_key, 6), position), (shards_of,), jnp.float32, smallest / len(cuts), high / len(cuts))
        loudness = loudness * jnp.repeat(jnp.exp(steps), dims[position] // shards_of).reshape((-1,) + (1,) * (len(dims) - 1 - position))
    return loudness


def centred(rng, dims, scale, limit, shards=(), kind=jnp.bfloat16):
    drawn = jax.random.normal(rng, dims, jnp.float32) * scale
    if len(shards) > 0:
        drawn = level_of(rng, dims, shards, -0.22, 0.18) * drawn
    return jnp.clip(drawn, min=-limit, max=limit).astype(kind)


def setup_inputs(seed: int = 0) -> dict:
    arg_keys = jax.random.split(jax.random.key(seed), 10)
    return {
        "queries": draw_queries(jax.random.fold_in(arg_keys[9], 71), 0),
        "local_keys": draw_local_keys(jax.random.fold_in(arg_keys[9], 71), 0),
        "local_values": centred(arg_keys[2], (TOKENS, HD), 1.0, 6.0, ((0, 512),)),
        "memory_keys": draw_memory_keys(jax.random.fold_in(arg_keys[9], 71), 0),
        "memory_values": centred(arg_keys[4], (MEM, HD), 1.0, 6.0, ((0, 16),)),
        "block_lists": draw_block_lists(jax.random.fold_in(arg_keys[9], 71), 0),
        "block_counts": touch_ends(jax.random.randint(arg_keys[6], (NQB,), 1, LIST + 1), jax.random.fold_in(arg_keys[6], 1), 1, LIST).astype(jnp.int32),
        "doc_starts": draw_doc_starts(jax.random.fold_in(arg_keys[9], 71), 0),
        "gate_bias": jnp.clip(jax.random.uniform(arg_keys[8], (H,), jnp.float32, -2.0, 2.0), -2.0, 2.0),
    }


def reference(queries, local_keys, local_values, memory_keys, memory_values, block_lists, block_counts, doc_starts, gate_bias):
    score_scale = float(HS) ** -0.5
    highest = lax.Precision.HIGHEST
    query_blocks = queries.reshape(NQB, QBLK, H, HS)
    memory_key_blocks = memory_keys.reshape(NBLK, MBLK, H, HS)
    memory_value_blocks = memory_values.reshape(NBLK, MBLK, H, HS)
    padded_keys = jnp.concatenate([jnp.zeros((WINDOW, HD), jnp.bfloat16), local_keys], axis=0)
    padded_values = jnp.concatenate([jnp.zeros((WINDOW, HD), jnp.bfloat16), local_values], axis=0)
    slot_index = jnp.arange(LIST, dtype=jnp.int32)
    slot_live = slot_index[None, :] < block_counts[:, None]
    repeated = (block_lists[:, :, None] == block_lists[:, None, :]) & slot_live[:, None, :] & (slot_index[None, None, :] < slot_index[None, :, None])
    first_live = slot_live & jnp.logical_not(jnp.any(repeated, axis=2))
    gate_share = jax.nn.sigmoid(gate_bias)[:, None, None]
    owner_index = jnp.arange(N_MEM, dtype=jnp.int32)

    def one_block(block_index):
        block_ids = block_lists[block_index]
        live_here = first_live[block_index]
        query_rows = query_blocks[block_index].astype(jnp.float32)
        key_rows = memory_key_blocks[block_ids].reshape(LIST * MBLK, H, HS).astype(jnp.float32)
        value_rows = memory_value_blocks[block_ids].reshape(LIST * MBLK, H, HS).astype(jnp.float32)
        scores = jnp.einsum('qhd,khd->hqk', query_rows, key_rows, precision=highest) * score_scale
        key_live = jnp.repeat(live_here, MBLK)
        key_owner = jnp.repeat(block_ids // BLK_DEV, MBLK)
        owned = (key_owner[None, :] == owner_index[:, None]) & key_live[None, :]
        owner_max = jnp.max(jnp.where(owned[:, None, None, :], scores[None], -1e30), axis=-1)
        key_max = jnp.transpose(owner_max[key_owner], (1, 2, 0))
        weights = jnp.where(key_live[None, None, :], jnp.exp(scores - key_max), 0.0)
        owned_float = owned.astype(jnp.float32)
        owner_total = jnp.einsum('ok,hqk->ohq', owned_float, weights, precision=highest)
        rounded = weights.astype(jnp.bfloat16).astype(jnp.float32)
        numerator = jnp.einsum('ok,hqk,khd->ohqd', owned_float, rounded, value_rows, precision=highest)
        safe_total = jnp.where(owner_total > 0, owner_total, 1.0)
        readout = (numerator / safe_total[..., None]).astype(jnp.bfloat16).astype(jnp.float32)
        largest = jnp.max(owner_max, axis=0)
        shares = owner_total * jnp.exp(owner_max - largest[None])
        memory_out = jnp.sum(shares[..., None] * readout, axis=0) / jnp.sum(shares, axis=0)[..., None]

        row_start = block_index * QBLK
        window_keys = lax.dynamic_slice_in_dim(padded_keys, row_start, WINDOW + QBLK, 0).reshape(WINDOW + QBLK, H, HS).astype(jnp.float32)
        window_values = lax.dynamic_slice_in_dim(padded_values, row_start, WINDOW + QBLK, 0).reshape(WINDOW + QBLK, H, HS).astype(jnp.float32)
        query_pos = row_start + jnp.arange(QBLK, dtype=jnp.int32)
        key_pos = row_start - WINDOW + jnp.arange(WINDOW + QBLK, dtype=jnp.int32)
        doc_first = jnp.max(jnp.where(doc_starts[None, :] <= query_pos[:, None], doc_starts[None, :], 0), axis=1)
        visible = (key_pos[None, :] <= query_pos[:, None]) & (query_pos[:, None] - key_pos[None, :] < WINDOW) & (key_pos[None, :] >= doc_first[:, None])
        local_scores = jnp.einsum('qhd,khd->hqk', query_rows, window_keys, precision=highest) * score_scale
        local_max = jnp.max(jnp.where(visible[None], local_scores, -1e30), axis=-1)
        local_weights = jnp.where(visible[None], jnp.exp(local_scores - local_max[..., None]), 0.0)
        local_total = jnp.sum(local_weights, axis=-1)
        local_rounded = local_weights.astype(jnp.bfloat16).astype(jnp.float32)
        local_out = jnp.einsum('hqk,khd->hqd', local_rounded, window_values, precision=highest) / local_total[..., None]
        mixed = gate_share * memory_out + (1.0 - gate_share) * local_out
        return jnp.transpose(mixed, (1, 0, 2)).reshape(QBLK, HD).astype(jnp.bfloat16)

    result = lax.map(one_block, jnp.arange(NQB, dtype=jnp.int32))
    return result.reshape(TOKENS, HD)
```

```python
import functools

import jax
import jax.numpy as jnp
from jax import lax
from jax.experimental import pallas as pl
from jax.experimental.pallas import tpu as pltpu
from jax.sharding import PartitionSpec as P

MESH = pl.DeviceIdType.MESH

WINDOW = 1024
QBLK = 64
MBLK = 64
LIST = 8
HS = 128
HEADS = 8
MASKED = -1e30
LOG2E = 1.4426950408889634


def kernel(
    n_seq, n_mem, tok, shard,
    q_ref, k_ref, v_ref, mk_ref, mv_ref, slots_ref, docs_ref, gate_ref,
    out_ref,
    qbuf, kvbuf, membuf, lbuf, obuf,
    q_send, kv_send, q_recv, kv_recv, halo_send, halo_recv,
    mem_send, mem_recv, swap_send, swap_recv, out_send, out_recv,
):
    s = lax.axis_index("seq")
    m = lax.axis_index("mem")
    core = lax.rem(s, 2)
    head = m // 2
    parity = lax.rem(m, 2)
    nxt = lax.rem(s + 1, n_seq)
    prv = lax.rem(s + n_seq - 1, n_seq)
    partner = s + 1 - 2 * core
    n_rank = n_mem // 2
    blocks = shard // MBLK
    spare = n_rank * blocks
    group = n_mem * tok

    barrier = pltpu.get_barrier_semaphore()

    def greet(i, c):
        t = lax.rem(m + 1 + i, n_mem)
        pl.semaphore_signal(barrier, inc=1, device_id={"seq": s, "mem": t}, device_id_type=MESH)
        return c

    lax.fori_loop(0, n_mem - 1, greet, 0)
    for other in (nxt, prv):
        pl.semaphore_signal(barrier, inc=1, device_id={"seq": other, "mem": m}, device_id_type=MESH)

    def q_src(t):
        first = QBLK * lax.rem(lax.rem(t, 2) + m, 2)
        return q_ref.at[pl.ds(pl.multiple_of(first, QBLK), QBLK), pl.ds(pl.multiple_of((t // 2) * HS, HS), HS)]

    def kv_src(ref, t):
        return ref.at[:, pl.ds(pl.multiple_of((t // 2) * HS, HS), HS)]

    q_dst = qbuf.at[pl.ds(pl.multiple_of(m * QBLK, QBLK), QBLK)]
    kv_rows = pl.ds(pl.multiple_of(WINDOW + m * tok, tok), tok)
    mem_rows = pl.ds(head * blocks, blocks)

    pltpu.make_async_copy(q_src(m), q_dst, q_recv).start()
    pltpu.make_async_copy(kv_src(k_ref, m), kvbuf.at[0, kv_rows], kv_recv).start()
    pltpu.make_async_copy(kv_src(v_ref, m), kvbuf.at[1, kv_rows], kv_recv).start()

    def mem_src(ref, h):
        return ref.at[:, :, pl.ds(pl.multiple_of(h * HS, HS), HS)]

    mem_dst = membuf.at[core, mem_rows]

    @pl.when(core == 0)
    def _():
        pltpu.make_async_copy(mem_src(mk_ref, head), mem_dst, mem_recv.at[head]).start()

    @pl.when(core == 1)
    def _():
        pltpu.make_async_copy(mem_src(mv_ref, head), mem_dst, mem_recv.at[head]).start()

    membuf[:, spare] = jnp.zeros((2, MBLK, HS), jnp.bfloat16)
    pl.semaphore_wait(barrier, n_mem + 1)

    def send_qkv(i, c):
        t = lax.rem(m + 1 + i, n_mem)
        to = {"seq": s, "mem": t}
        pltpu.make_async_remote_copy(q_src(t), q_dst, q_send, q_recv, to, MESH).start()
        pltpu.make_async_remote_copy(kv_src(k_ref, t), kvbuf.at[0, kv_rows], kv_send, kv_recv, to, MESH).start()
        pltpu.make_async_remote_copy(kv_src(v_ref, t), kvbuf.at[1, kv_rows], kv_send, kv_recv, to, MESH).start()
        return c

    lax.fori_loop(0, n_mem - 1, send_qkv, 0)

    def send_mem(ref):
        def body(i, c):
            h = lax.rem(head + 1 + i, HEADS)
            to = {"seq": s, "mem": 2 * h + parity}
            pltpu.make_async_remote_copy(mem_src(ref, h), mem_dst, mem_send, mem_recv.at[head], to, MESH).start()
            return c

        lax.fori_loop(0, HEADS - 1, body, 0)

    @pl.when(core == 0)
    def _():
        send_mem(mk_ref)

    @pl.when(core == 1)
    def _():
        send_mem(mv_ref)

    def arrived(ref, sem):
        pltpu.make_async_copy(ref, ref, sem).wait()

    arrived(qbuf, q_recv)
    arrived(kvbuf.at[:, pl.ds(WINDOW, group)], kv_recv)
    halo = pltpu.make_async_remote_copy(
        kvbuf.at[:, pl.ds(group, WINDOW)], kvbuf.at[:, pl.ds(0, WINDOW)], halo_send, halo_recv,
        {"seq": nxt, "mem": m}, MESH,
    )
    halo.start()

    coef = float(HS) ** -0.5 * LOG2E
    keys = WINDOW + tok

    def half_of(b):
        return lax.rem(parity + b, 2)

    def local_block(b):
        q = qbuf[pl.ds(pl.multiple_of(b * QBLK, QBLK), QBLK), :]
        rows = pl.ds(pl.multiple_of(b * tok, tok), keys)
        sc = lax.dot_general(q, kvbuf[0, rows, :], (((1,), (1,)), ((), ())), preferred_element_type=jnp.float32)
        base = s * group + b * tok - WINDOW
        trel = WINDOW + QBLK * half_of(b) + lax.broadcasted_iota(jnp.int32, (QBLK, 1), 0)
        tpos = base + trel
        first = jnp.zeros((QBLK, 1), jnp.int32)
        for d in range(docs_ref.shape[0]):
            start = docs_ref[d]
            first = jnp.maximum(first, jnp.where(start <= tpos, start, 0))
        low = jnp.maximum(first - base, trel - (WINDOW - 1))
        col = lax.broadcasted_iota(jnp.int32, (QBLK, keys), 1)
        sc = jnp.where((col >= low) & (col <= trel), sc, MASKED)
        top = jnp.max(sc, axis=1, keepdims=True)
        w = jnp.exp2((sc - top) * coef)
        total = jnp.sum(w, axis=1, keepdims=True)
        acc = jnp.dot(w.astype(jnp.bfloat16), kvbuf[1, rows, :], preferred_element_type=jnp.float32)
        lbuf[pl.ds(pl.multiple_of(b * QBLK, QBLK), QBLK), :] = acc / total

    def local_range(lo, hi):
        def body(b, c):
            local_block(b)
            return c

        lax.fori_loop(lo, hi, body, 0)

    reach = WINDOW // tok
    local_range(reach, n_mem)

    def pass_on(r, c):
        piece = membuf.at[core, pl.ds(r * blocks, blocks)]
        arrived(piece, mem_recv.at[r])
        pltpu.make_async_remote_copy(piece, piece, swap_send, swap_recv, {"seq": partner, "mem": m}, MESH).start()
        return c

    lax.fori_loop(0, n_rank, pass_on, 0)

    halo.wait_recv()
    local_range(0, reach)

    arrived(membuf.at[1 - core, pl.ds(0, spare)], swap_recv)

    gate = jnp.full((1, HS), gate_ref[head], jnp.float32)
    gate = 1.0 / (1.0 + jnp.exp(-gate))
    lane_slot = lax.broadcasted_iota(jnp.int32, (1, LIST * MBLK), 1) // MBLK

    def out_copy(b):
        src = obuf.at[pl.ds(pl.multiple_of(b * QBLK, QBLK), QBLK)]
        return src

    out_rows_of = lambda b: pl.ds(pl.multiple_of(QBLK * half_of(b), QBLK), QBLK)
    out_cols = pl.ds(pl.multiple_of(head * HS, HS), HS)

    def mem_block(i, c):
        b = lax.rem(m + 1 + i, n_mem)
        row = 2 * b + half_of(b)
        place = jnp.zeros((1, LIST * MBLK), jnp.int32)
        for j in range(LIST):
            place = jnp.where(lane_slot == j, slots_ref[j, row], place)
        places = [slots_ref[j, row] for j in range(LIST)]
        q = qbuf[pl.ds(pl.multiple_of(b * QBLK, QBLK), QBLK), :]
        kk = jnp.concatenate([membuf[0, x] for x in places], axis=0)
        vv = jnp.concatenate([membuf[1, x] for x in places], axis=0)
        sc = lax.dot_general(q, kk, (((1,), (1,)), ((), ())), preferred_element_type=jnp.float32)
        sc = jnp.where(place < spare, sc, MASKED)
        top = jnp.max(sc, axis=1, keepdims=True)
        w = jnp.exp2((sc - top) * coef)
        total = jnp.sum(w, axis=1, keepdims=True)
        acc = jnp.dot(w.astype(jnp.bfloat16), vv, preferred_element_type=jnp.float32)
        rows = pl.ds(pl.multiple_of(b * QBLK, QBLK), QBLK)
        obuf[rows, :] = (gate * (acc / total) + (1.0 - gate) * lbuf[rows, :]).astype(jnp.bfloat16)
        dst = out_ref.at[out_rows_of(m), out_cols]

        @pl.when(b != m)
        def _():
            pltpu.make_async_remote_copy(
                obuf.at[rows], out_ref.at[out_rows_of(b), out_cols], out_send, out_recv,
                {"seq": s, "mem": b}, MESH,
            ).start()

        @pl.when(b == m)
        def _():
            pltpu.make_async_copy(obuf.at[rows], dst, out_recv).start()

        return c

    lax.fori_loop(0, n_mem, mem_block, 0)

    arrived(out_ref, out_recv)
    arrived(qbuf.at[pl.ds(0, (n_mem - 1) * QBLK)], q_send)
    arrived(kvbuf.at[:, pl.ds(0, (n_mem - 1) * tok)], kv_send)
    halo.wait_send()
    arrived(membuf.at[0, pl.ds(0, (HEADS - 1) * blocks)], mem_send)
    arrived(membuf.at[0, pl.ds(0, spare)], swap_send)
    arrived(obuf.at[pl.ds(0, (n_mem - 1) * QBLK)], out_send)


def list_slots(lists, counts, blocks, spare):
    lists = lists.T
    place = lists // (2 * blocks) * blocks + lists % blocks
    slot = jnp.arange(LIST, dtype=jnp.int32)
    earlier = (slot[None, :] < slot[:, None])[:, :, None]
    repeats = jnp.any((lists[:, None, :] == lists[None, :, :]) & earlier, axis=1)
    return jnp.where((slot[:, None] < counts[None, :]) & ~repeats, place, spare)


def solution(mesh):
    n_seq, n_mem = mesh.shape["seq"], mesh.shape["mem"]

    def on_device(q, k, v, mk, mv, lists, counts, docs, gate):
        tok, width = q.shape
        shard = mk.shape[0]
        group = n_mem * tok
        spare = n_mem // 2 * shard // MBLK
        by_block = lambda x: x.reshape(shard // MBLK, MBLK, width)
        hbm = pl.BlockSpec(memory_space=pl.ANY)
        smem = pl.BlockSpec(memory_space=pltpu.SMEM)
        dma = pltpu.SemaphoreType.DMA
        return pl.pallas_call(
            functools.partial(kernel, n_seq, n_mem, tok, shard),
            out_shape=jax.ShapeDtypeStruct((tok, width), jnp.bfloat16),
            in_specs=[hbm] * 5 + [smem] * 3,
            out_specs=hbm,
            scratch_shapes=[
                pltpu.VMEM((n_mem * QBLK, HS), jnp.bfloat16),
                pltpu.VMEM((2, WINDOW + group, HS), jnp.bfloat16),
                pltpu.VMEM((2, spare + 1, MBLK, HS), jnp.bfloat16),
                pltpu.VMEM((n_mem * QBLK, HS), jnp.float32),
                pltpu.VMEM((n_mem * QBLK, HS), jnp.bfloat16),
                dma, dma, dma, dma, dma, dma,
                dma, dma((n_mem // 2,)), dma, dma, dma, dma,
            ],
            compiler_params=pltpu.CompilerParams(
                collective_id=0, has_side_effects=True, vmem_limit_bytes=56 * 1024 * 1024
            ),
            name="memorizing_attention",
        )(q, k, v, by_block(mk), by_block(mv), list_slots(lists, counts, shard // MBLK, spare), docs, gate)

    in_specs = (
        P(("seq", "mem"), None),
        P(("seq", "mem"), None),
        P(("seq", "mem"), None),
        P("mem", None),
        P("mem", None),
        P("seq", None),
        P("seq"),
        P(),
        P(),
    )
    return jax.shard_map(
        on_device, mesh=mesh, in_specs=in_specs, out_specs=P(("seq", "mem"), None), check_vma=False
    )
```

```python
import functools

import jax
import jax.numpy as jnp
from jax import lax
from jax.experimental import pallas as pl
from jax.experimental.pallas import tpu as pltpu
from jax.sharding import PartitionSpec as P

MESH = pl.DeviceIdType.MESH

WINDOW = 1024
QBLK = 64
MBLK = 64
LIST = 8
HS = 128
HEADS = 8
BATCH = 4
MASKED = -1e30
LOG2E = 1.4426950408889634
COEF = float(HS) ** -0.5 * LOG2E


def aligned(first, size):
    return pl.ds(pl.multiple_of(first, size), size)


def arrived(ref, sem):
    pltpu.make_async_copy(ref, ref, sem).wait()


def kernel(
    n_seq, n_mem, tok, shard,
    q_ref, k_ref, v_ref, mk_ref, mv_ref, lists_ref, counts_ref, docs_ref, gate_ref,
    out_ref,
    qbuf, kvbuf, membuf, mixed, obuf, lists, counts, slots_vmem, slots, docs, gates,
    small_sem, slot_sem, q_send, kv_send, q_recv, kv_recv, halo_send, halo_recv,
    mem_send, mem_recv, z_send, z_recv, swap_send, swap_recv, out_send, out_recv,
):
    s = lax.axis_index("seq")
    m = lax.axis_index("mem")
    core = lax.rem(s, 2)
    z_half = lax.rem(s // 2, 2)
    head = m // 2
    parity = lax.rem(m, 2)
    nxt = {"seq": lax.rem(s + 1, n_seq), "mem": m}
    prv = {"seq": lax.rem(s + n_seq - 1, n_seq), "mem": m}
    up = {"seq": lax.rem(s + 2, n_seq), "mem": m}
    down = {"seq": lax.rem(s + n_seq - 2, n_seq), "mem": m}
    along_z = {"seq": lax.rem(s + 2 - 4 * core + n_seq, n_seq), "mem": m}
    partner = {"seq": s + 1 - 2 * core, "mem": m}
    n_rank = n_mem // 2
    blocks = shard // MBLK
    half = blocks // 2
    spare = n_rank * blocks
    group = n_mem * tok

    smalls = (
        pltpu.make_async_copy(lists_ref, lists, small_sem.at[0]),
        pltpu.make_async_copy(counts_ref, counts, small_sem.at[1]),
        pltpu.make_async_copy(docs_ref, docs, small_sem.at[2]),
        pltpu.make_async_copy(gate_ref, gates, small_sem.at[3]),
    )
    for copy in smalls:
        copy.start()

    barrier = pltpu.get_barrier_semaphore()

    def greet(i, c):
        t = lax.rem(m + 1 + i, n_mem)
        pl.semaphore_signal(barrier, inc=1, device_id={"seq": s, "mem": t}, device_id_type=MESH)
        return c

    lax.fori_loop(0, n_mem - 1, greet, 0)
    for other in (nxt, prv, up, down):
        pl.semaphore_signal(barrier, inc=1, device_id=other, device_id_type=MESH)

    def cols(h):
        return aligned(h * HS, HS)

    def q_src(t):
        first = QBLK * lax.rem(lax.rem(t, 2) + m, 2)
        return q_ref.at[aligned(first, QBLK), cols(t // 2)]

    def kv_src(ref, t):
        return ref.at[:, cols(t // 2)]

    def mem_src(ref, h):
        return ref.at[pl.ds(z_half * half, half), :, cols(h)]

    def piece(r, z):
        return membuf.at[core, pl.ds(r * blocks + z * half, half)]

    def kv_rows(src):
        return aligned(WINDOW + src * tok, tok)

    q_dst = qbuf.at[aligned(m * QBLK, QBLK)]
    mem_dst = piece(head, z_half)
    for on_core, ref in ((0, mk_ref), (1, mv_ref)):

        @pl.when(core == on_core)
        def _(ref=ref):
            pltpu.make_async_copy(mem_src(ref, head), mem_dst, mem_recv.at[head]).start()

    pltpu.make_async_copy(q_src(m), q_dst, q_recv).start()
    for kind, ref in enumerate((k_ref, v_ref)):
        pltpu.make_async_copy(kv_src(ref, m), kvbuf.at[kind, kv_rows(m)], kv_recv.at[m]).start()

    membuf[:, spare] = jnp.zeros((2, MBLK, HS), jnp.bfloat16)
    pl.semaphore_wait(barrier, n_mem + 3)

    for on_core, ref in ((0, mk_ref), (1, mv_ref)):

        @pl.when(core == on_core)
        def _(ref=ref):
            def body(i, c):
                h = lax.rem(head + 1 + i, HEADS)
                to = {"seq": s, "mem": 2 * h + parity}
                pltpu.make_async_remote_copy(
                    mem_src(ref, h), mem_dst, mem_send, mem_recv.at[head], to, MESH
                ).start()
                return c

            lax.fori_loop(0, HEADS - 1, body, 0)

    def send_q(i, c):
        t = lax.rem(m + 1 + i, n_mem)
        to = {"seq": s, "mem": t}
        pltpu.make_async_remote_copy(q_src(t), q_dst, q_send, q_recv, to, MESH).start()
        return c

    lax.fori_loop(0, n_mem - 1, send_q, 0)

    def send_kv(i, c):
        t = lax.rem(m + 1 + i, n_mem)
        to = {"seq": s, "mem": t}
        for kind, ref in enumerate((k_ref, v_ref)):
            pltpu.make_async_remote_copy(
                kv_src(ref, t), kvbuf.at[kind, kv_rows(m)], kv_send, kv_recv.at[m], to, MESH
            ).start()
        return c

    lax.fori_loop(0, n_mem - 1, send_kv, 0)

    for copy in smalls:
        copy.wait()
    named = [lists[j : j + 1, :] for j in range(LIST)]
    for j in range(LIST):
        ok = j < counts[...]
        for e in range(j):
            ok = ok & (named[e] != named[j])
        place = lax.shift_right_logical(named[j], 4) * blocks + (named[j] & (blocks - 1))
        slots_vmem[j : j + 1, :] = jnp.where(ok, place, spare)
    to_slots = pltpu.make_async_copy(slots_vmem, slots, slot_sem)
    to_slots.start()

    def pass_first(i, c):
        r = lax.rem(head + n_rank - i, n_rank)
        got = piece(r, z_half)
        arrived(got, mem_recv.at[r])
        pltpu.make_async_remote_copy(got, got, z_send, z_recv.at[r], along_z, MESH).start()
        pltpu.make_async_remote_copy(got, got, swap_send, swap_recv, partner, MESH).start()
        return c

    lax.fori_loop(0, n_rank, pass_first, 0)

    def pass_second(i, c):
        r = lax.rem(head + n_rank - i, n_rank)
        got = piece(r, 1 - z_half)
        arrived(got, z_recv.at[r])
        pltpu.make_async_remote_copy(got, got, swap_send, swap_recv, partner, MESH).start()
        return c

    lax.fori_loop(0, n_rank, pass_second, 0)

    to_slots.wait()
    arrived(qbuf, q_recv)
    arrived(membuf.at[1 - core, pl.ds(0, spare)], swap_recv)

    gate = 1.0 / (1.0 + jnp.exp(-jnp.full((1, HS), gates[head], jnp.float32)))
    lane_slot = lax.broadcasted_iota(jnp.int32, (1, LIST * MBLK), 1) // MBLK

    def half_of(b):
        return lax.rem(parity + b, 2)

    def softmax(sc):
        w = jnp.exp2((sc - jnp.max(sc, axis=1, keepdims=True)) * COEF)
        return w.astype(jnp.bfloat16), jnp.sum(w, axis=1, keepdims=True)

    def scores(q, k):
        return lax.dot_general(q, k, (((1,), (1,)), ((), ())), preferred_element_type=jnp.float32)

    def mem_block(b, c):
        row = 2 * b + half_of(b)
        place = jnp.zeros((1, LIST * MBLK), jnp.int32)
        for j in range(LIST):
            place = jnp.where(lane_slot == j, slots[j, row], place)
        places = [slots[j, row] for j in range(LIST)]
        rows = aligned(b * QBLK, QBLK)
        kk = jnp.concatenate([membuf[0, x] for x in places], axis=0)
        vv = jnp.concatenate([membuf[1, x] for x in places], axis=0)
        w, total = softmax(jnp.where(place < spare, scores(qbuf[rows, :], kk), MASKED))
        mixed[rows, :] = gate * (jnp.dot(w, vv, preferred_element_type=jnp.float32) / total)
        return c

    lax.fori_loop(0, n_mem, mem_block, 0, unroll=2)

    reach = WINDOW // tok

    def pass_halo(i, c):
        src = lax.rem(m + n_mem - i, n_mem)
        arrived(kvbuf.at[:, kv_rows(src)], kv_recv.at[src])

        @pl.when(src >= n_mem - reach)
        def _():
            dst = kvbuf.at[:, aligned((src - (n_mem - reach)) * tok, tok)]
            pltpu.make_async_remote_copy(
                kvbuf.at[:, kv_rows(src)], dst, halo_send, halo_recv, nxt, MESH
            ).start()

        return c

    lax.fori_loop(0, n_mem, pass_halo, 0)

    keys = WINDOW + BATCH * tok
    batches = n_mem // BATCH

    def local_batch(i, c):
        b = BATCH * i
        rows = aligned(b * QBLK, BATCH * QBLK)
        span = pl.ds(pl.multiple_of(b * tok, tok), keys)
        sc = scores(qbuf[rows, :], kvbuf[0, span, :])
        row = lax.broadcasted_iota(jnp.int32, (BATCH * QBLK, 1), 0)
        block = row // QBLK
        until = WINDOW + block * tok + QBLK * lax.rem(parity + block, 2) + lax.rem(row, QBLK)
        base = s * group + b * tok - WINDOW
        token = base + until
        first = jnp.zeros((BATCH * QBLK, 1), jnp.int32)
        for d in range(docs_ref.shape[0]):
            start = docs[d]
            first = jnp.maximum(first, jnp.where(start <= token, start, 0))
        low = jnp.maximum(first - base, until - (WINDOW - 1))
        col = lax.broadcasted_iota(jnp.int32, (BATCH * QBLK, keys), 1)
        sc = jnp.where(col >= low, sc, MASKED)
        tail = jnp.where(col[:, WINDOW:] <= until, sc[:, WINDOW:], MASKED)
        w, total = softmax(jnp.concatenate([sc[:, :WINDOW], tail], axis=1))
        local = jnp.dot(w, kvbuf[1, span, :], preferred_element_type=jnp.float32) / total
        obuf[rows, :] = (mixed[rows, :] + (1.0 - gate) * local).astype(jnp.bfloat16)
        for j in range(BATCH):
            t = b + j
            src = obuf.at[aligned(t * QBLK, QBLK)]
            dst = out_ref.at[aligned(QBLK * half_of(t), QBLK), cols(head)]

            @pl.when(t != m)
            def _():
                pltpu.make_async_remote_copy(
                    src, dst, out_send, out_recv, {"seq": s, "mem": t}, MESH
                ).start()

            @pl.when(t == m)
            def _():
                pltpu.make_async_copy(src, dst, out_recv).start()

        return c

    lax.fori_loop(batches // 2, batches, local_batch, 0)
    arrived(kvbuf.at[:, pl.ds(0, WINDOW)], halo_recv)
    lax.fori_loop(0, batches // 2, local_batch, 0)

    arrived(mem_dst_all(membuf, 0, (HEADS - 1) * half), mem_send)
    arrived(mem_dst_all(membuf, 0, n_rank * half), z_send)
    arrived(mem_dst_all(membuf, 0, spare), swap_send)
    arrived(qbuf.at[pl.ds(0, (n_mem - 1) * QBLK)], q_send)
    arrived(kvbuf.at[:, pl.ds(0, (n_mem - 1) * tok)], kv_send)
    arrived(kvbuf.at[:, pl.ds(0, WINDOW)], halo_send)
    arrived(obuf.at[pl.ds(0, (n_mem - 1) * QBLK)], out_send)
    arrived(out_ref, out_recv)


def mem_dst_all(membuf, kind, count):
    return membuf.at[kind, pl.ds(0, count)]


def solution(mesh):
    n_seq, n_mem = mesh.shape["seq"], mesh.shape["mem"]

    def on_device(q, k, v, mk, mv, lists, counts, docs, gate):
        tok, width = q.shape
        shard = mk.shape[0]
        group = n_mem * tok
        spare = n_mem // 2 * shard // MBLK
        lists = lists.T
        counts = counts.reshape(1, -1)
        by_block = lambda x: x.reshape(shard // MBLK, MBLK, width)
        hbm = pl.BlockSpec(memory_space=pl.ANY)
        dma = pltpu.SemaphoreType.DMA
        return pl.pallas_call(
            functools.partial(kernel, n_seq, n_mem, tok, shard),
            out_shape=jax.ShapeDtypeStruct((tok, width), jnp.bfloat16),
            in_specs=[hbm] * 9,
            out_specs=hbm,
            scratch_shapes=[
                pltpu.VMEM((n_mem * QBLK, HS), jnp.bfloat16),
                pltpu.VMEM((2, WINDOW + group, HS), jnp.bfloat16),
                pltpu.VMEM((2, spare + 1, MBLK, HS), jnp.bfloat16),
                pltpu.VMEM((n_mem * QBLK, HS), jnp.float32),
                pltpu.VMEM((n_mem * QBLK, HS), jnp.bfloat16),
                pltpu.VMEM(lists.shape, jnp.int32),
                pltpu.VMEM(counts.shape, jnp.int32),
                pltpu.VMEM(lists.shape, jnp.int32),
                pltpu.SMEM(lists.shape, jnp.int32),
                pltpu.SMEM(docs.shape, jnp.int32),
                pltpu.SMEM(gate.shape, jnp.float32),
                dma((4,)), dma, dma, dma, dma, dma((n_mem,)), dma, dma,
                dma, dma((n_mem // 2,)), dma, dma((n_mem // 2,)), dma, dma, dma, dma,
            ],
            compiler_params=pltpu.CompilerParams(
                collective_id=0, has_side_effects=True, vmem_limit_bytes=56 * 1024 * 1024
            ),
            name="memorizing_attention",
        )(q, k, v, by_block(mk), by_block(mv), lists, counts, docs, gate)

    in_specs = (
        P(("seq", "mem"), None),
        P(("seq", "mem"), None),
        P(("seq", "mem"), None),
        P("mem", None),
        P("mem", None),
        P("seq", None),
        P("seq"),
        P(),
        P(),
    )
    return jax.shard_map(
        on_device, mesh=mesh, in_specs=in_specs, out_specs=P(("seq", "mem"), None), check_vma=False
    )
```

```python
import functools

import jax
import jax.numpy as jnp
from jax import lax
from jax.experimental import pallas as pl
from jax.experimental.pallas import tpu as pltpu
from jax.sharding import PartitionSpec as P

MESH = pl.DeviceIdType.MESH

WINDOW = 1024
QBLK = 64
MBLK = 64
LIST = 8
HS = 128
HEADS = 8
BATCH = 4
MASKED = -1e30
LOG2E = 1.4426950408889634
COEF = float(HS) ** -0.5 * LOG2E


def aligned(first, size):
    return pl.ds(pl.multiple_of(first, size), size)


def arrived(ref, sem):
    pltpu.make_async_copy(ref, ref, sem).wait()


def kernel(
    n_seq, n_mem, tok, shard,
    q_ref, k_ref, v_ref, mk_ref, mv_ref, lists_ref, counts_ref, docs_ref, gate_ref,
    out_ref,
    qbuf, kvbuf, membuf, mixed, obuf, lists, counts, slots_vmem, slots, docs, gates,
    small_sem, slot_sem, q_send, kv_send, q_recv, kv_recv, halo_send, halo_recv,
    mem_send, mem_recv, z_send, z_recv, swap_send, swap_recv, out_send, out_recv,
):
    s = lax.axis_index("seq")
    m = lax.axis_index("mem")
    core = lax.rem(s, 2)
    z_half = lax.rem(s // 2, 2)
    head = m // 2
    parity = lax.rem(m, 2)
    has_prv, has_nxt = s > 0, s < n_seq - 1
    nxt = {"seq": s + 1, "mem": m}
    prv = {"seq": s - 1, "mem": m}
    along_z = {"seq": s + 2 - 4 * z_half, "mem": m}
    partner = {"seq": s + 1 - 2 * core, "mem": m}
    n_rank = n_mem // 2
    blocks = shard // MBLK
    half = blocks // 2
    spare = n_rank * blocks
    group = n_mem * tok

    smalls = (
        pltpu.make_async_copy(lists_ref, lists, small_sem.at[0]),
        pltpu.make_async_copy(counts_ref, counts, small_sem.at[1]),
        pltpu.make_async_copy(docs_ref, docs, small_sem.at[2]),
        pltpu.make_async_copy(gate_ref, gates, small_sem.at[3]),
    )
    for copy in smalls:
        copy.start()

    barrier = pltpu.get_barrier_semaphore()

    def greet(i, c):
        t = lax.rem(m + 1 + i, n_mem)
        pl.semaphore_signal(barrier, inc=1, device_id={"seq": s, "mem": t}, device_id_type=MESH)
        return c

    lax.fori_loop(0, n_mem - 1, greet, 0)
    for there, other in ((has_nxt, nxt), (has_prv, prv), (s >= 0, along_z)):

        @pl.when(there)
        def _(other=other):
            pl.semaphore_signal(barrier, inc=1, device_id=other, device_id_type=MESH)

    def cols(h):
        return aligned(h * HS, HS)

    def q_src(t):
        first = QBLK * lax.rem(lax.rem(t, 2) + m, 2)
        return q_ref.at[aligned(first, QBLK), cols(t // 2)]

    def kv_src(ref, t):
        return ref.at[:, cols(t // 2)]

    def mem_src(ref, h):
        return ref.at[pl.ds(z_half * half, half), :, cols(h)]

    def piece(r, z):
        return membuf.at[core, pl.ds(r * blocks + z * half, half)]

    def kv_rows(src):
        return aligned(WINDOW + src * tok, tok)

    q_dst = qbuf.at[aligned(m * QBLK, QBLK)]
    mem_dst = piece(head, z_half)
    for on_core, ref in ((0, mk_ref), (1, mv_ref)):

        @pl.when(core == on_core)
        def _(ref=ref):
            pltpu.make_async_copy(mem_src(ref, head), mem_dst, mem_recv.at[head]).start()

    pltpu.make_async_copy(q_src(m), q_dst, q_recv).start()
    for kind, ref in enumerate((k_ref, v_ref)):
        pltpu.make_async_copy(kv_src(ref, m), kvbuf.at[kind, kv_rows(m)], kv_recv.at[m]).start()

    membuf[:, spare] = jnp.zeros((2, MBLK, HS), jnp.bfloat16)

    @pl.when(jnp.logical_not(has_prv))
    def _():
        kvbuf[:, :WINDOW] = jnp.zeros((2, WINDOW, HS), jnp.bfloat16)

    inner = has_prv & has_nxt

    @pl.when(inner)
    def _():
        pl.semaphore_wait(barrier, n_mem + 2)

    @pl.when(jnp.logical_not(inner))
    def _():
        pl.semaphore_wait(barrier, n_mem + 1)

    for on_core, ref in ((0, mk_ref), (1, mv_ref)):

        @pl.when(core == on_core)
        def _(ref=ref):
            def body(i, c):
                h = lax.rem(head + 1 + i, HEADS)
                to = {"seq": s, "mem": 2 * h + parity}
                pltpu.make_async_remote_copy(
                    mem_src(ref, h), mem_dst, mem_send, mem_recv.at[head], to, MESH
                ).start()
                return c

            lax.fori_loop(0, HEADS - 1, body, 0)

    def send_q(i, c):
        t = lax.rem(m + 1 + i, n_mem)
        to = {"seq": s, "mem": t}
        pltpu.make_async_remote_copy(q_src(t), q_dst, q_send, q_recv, to, MESH).start()
        return c

    lax.fori_loop(0, n_mem - 1, send_q, 0)

    def send_kv(i, c):
        t = lax.rem(m + 1 + i, n_mem)
        to = {"seq": s, "mem": t}
        for kind, ref in enumerate((k_ref, v_ref)):
            pltpu.make_async_remote_copy(
                kv_src(ref, t), kvbuf.at[kind, kv_rows(m)], kv_send, kv_recv.at[m], to, MESH
            ).start()
        return c

    lax.fori_loop(0, n_mem - 1, send_kv, 0)

    for copy in smalls:
        copy.wait()
    named = [lists[j : j + 1, :] for j in range(LIST)]
    for j in range(LIST):
        ok = j < counts[...]
        for e in range(j):
            ok = ok & (named[e] != named[j])
        place = lax.shift_right_logical(named[j], 4) * blocks + (named[j] & (blocks - 1))
        slots_vmem[j : j + 1, :] = jnp.where(ok, place, spare)
    to_slots = pltpu.make_async_copy(slots_vmem, slots, slot_sem)
    to_slots.start()

    def pass_first(i, c):
        r = lax.rem(head + n_rank - i, n_rank)
        got = piece(r, z_half)
        arrived(got, mem_recv.at[r])
        pltpu.make_async_remote_copy(got, got, z_send, z_recv.at[r], along_z, MESH).start()
        pltpu.make_async_remote_copy(got, got, swap_send, swap_recv, partner, MESH).start()
        return c

    lax.fori_loop(0, n_rank, pass_first, 0)

    def pass_second(i, c):
        r = lax.rem(head + n_rank - i, n_rank)
        got = piece(r, 1 - z_half)
        arrived(got, z_recv.at[r])
        pltpu.make_async_remote_copy(got, got, swap_send, swap_recv, partner, MESH).start()
        return c

    lax.fori_loop(0, n_rank, pass_second, 0)

    gate = 1.0 / (1.0 + jnp.exp(-jnp.full((1, HS), gates[head], jnp.float32)))
    lane_slot = lax.broadcasted_iota(jnp.int32, (1, LIST * MBLK), 1) // MBLK

    def half_of(b):
        return lax.rem(parity + b, 2)

    def softmax(sc):
        w = jnp.exp2((sc - jnp.max(sc, axis=1, keepdims=True)) * COEF)
        return w.astype(jnp.bfloat16), jnp.sum(w, axis=1, keepdims=True)

    def scores(q, k):
        return lax.dot_general(q, k, (((1,), (1,)), ((), ())), preferred_element_type=jnp.float32)

    def mem_block(b, c):
        row = 2 * b + half_of(b)
        place = jnp.zeros((1, LIST * MBLK), jnp.int32)
        for j in range(LIST):
            place = jnp.where(lane_slot == j, slots[j, row], place)
        places = [slots[j, row] for j in range(LIST)]
        rows = aligned(b * QBLK, QBLK)
        kk = jnp.concatenate([membuf[0, x] for x in places], axis=0)
        vv = jnp.concatenate([membuf[1, x] for x in places], axis=0)
        w, total = softmax(jnp.where(place < spare, scores(qbuf[rows, :], kk), MASKED))
        mixed[rows, :] = gate * (jnp.dot(w, vv, preferred_element_type=jnp.float32) / total)
        return c


    reach = WINDOW // tok

    late = n_mem - reach

    def take(src):
        arrived(kvbuf.at[:, kv_rows(src)], kv_recv.at[src])

    def pass_halo(i, c):
        place = lax.rem(m + n_mem - i, reach)
        src = late + place
        take(src)

        @pl.when(has_nxt)
        def _():
            dst = kvbuf.at[:, aligned(place * tok, tok)]
            pltpu.make_async_remote_copy(
                kvbuf.at[:, kv_rows(src)], dst, halo_send, halo_recv, nxt, MESH
            ).start()

        return c

    lax.fori_loop(0, reach, pass_halo, 0)
    to_slots.wait()
    arrived(qbuf, q_recv)
    arrived(membuf.at[1 - core, pl.ds(0, spare)], swap_recv)
    lax.fori_loop(0, n_mem, mem_block, 0, unroll=2)

    def take_rest(src, c):
        take(src)
        return c

    lax.fori_loop(0, late, take_rest, 0)

    keys = WINDOW + BATCH * tok
    batches = n_mem // BATCH

    def local_batch(i, c):
        b = BATCH * i
        rows = aligned(b * QBLK, BATCH * QBLK)
        span = pl.ds(pl.multiple_of(b * tok, tok), keys)
        sc = scores(qbuf[rows, :], kvbuf[0, span, :])
        row = lax.broadcasted_iota(jnp.int32, (BATCH * QBLK, 1), 0)
        block = row // QBLK
        until = WINDOW + block * tok + QBLK * lax.rem(parity + block, 2) + lax.rem(row, QBLK)
        base = s * group + b * tok - WINDOW
        token = base + until
        first = jnp.zeros((BATCH * QBLK, 1), jnp.int32)
        for d in range(docs_ref.shape[0]):
            start = docs[d]
            first = jnp.maximum(first, jnp.where(start <= token, start, 0))
        low = jnp.maximum(first - base, until - (WINDOW - 1))
        col = lax.broadcasted_iota(jnp.int32, (BATCH * QBLK, keys), 1)
        sc = jnp.where(col >= low, sc, MASKED)
        tail = jnp.where(col[:, WINDOW:] <= until, sc[:, WINDOW:], MASKED)
        w, total = softmax(jnp.concatenate([sc[:, :WINDOW], tail], axis=1))
        local = jnp.dot(w, kvbuf[1, span, :], preferred_element_type=jnp.float32) / total
        obuf[rows, :] = (mixed[rows, :] + (1.0 - gate) * local).astype(jnp.bfloat16)
        for j in range(BATCH):
            t = b + j
            src = obuf.at[aligned(t * QBLK, QBLK)]
            dst = out_ref.at[aligned(QBLK * half_of(t), QBLK), cols(head)]

            @pl.when(t != m)
            def _():
                pltpu.make_async_remote_copy(
                    src, dst, out_send, out_recv, {"seq": s, "mem": t}, MESH
                ).start()

            @pl.when(t == m)
            def _():
                pltpu.make_async_copy(src, dst, out_recv).start()

        return c

    lax.fori_loop(batches // 2, batches, local_batch, 0)

    @pl.when(has_prv)
    def _():
        arrived(kvbuf.at[:, pl.ds(0, WINDOW)], halo_recv)

    lax.fori_loop(0, batches // 2, local_batch, 0)

    arrived(mem_dst_all(membuf, 0, (HEADS - 1) * half), mem_send)
    arrived(mem_dst_all(membuf, 0, n_rank * half), z_send)
    arrived(mem_dst_all(membuf, 0, spare), swap_send)
    arrived(qbuf.at[pl.ds(0, (n_mem - 1) * QBLK)], q_send)
    arrived(kvbuf.at[:, pl.ds(0, (n_mem - 1) * tok)], kv_send)

    @pl.when(has_nxt)
    def _():
        arrived(kvbuf.at[:, pl.ds(0, WINDOW)], halo_send)

    arrived(obuf.at[pl.ds(0, (n_mem - 1) * QBLK)], out_send)
    arrived(out_ref, out_recv)


def mem_dst_all(membuf, kind, count):
    return membuf.at[kind, pl.ds(0, count)]


def solution(mesh):
    n_seq, n_mem = mesh.shape["seq"], mesh.shape["mem"]

    def on_device(q, k, v, mk, mv, lists, counts, docs, gate):
        tok, width = q.shape
        shard = mk.shape[0]
        group = n_mem * tok
        spare = n_mem // 2 * shard // MBLK
        lists = lists.T
        counts = counts.reshape(1, -1)
        by_block = lambda x: x.reshape(shard // MBLK, MBLK, width)
        hbm = pl.BlockSpec(memory_space=pl.ANY)
        dma = pltpu.SemaphoreType.DMA
        return pl.pallas_call(
            functools.partial(kernel, n_seq, n_mem, tok, shard),
            out_shape=jax.ShapeDtypeStruct((tok, width), jnp.bfloat16),
            in_specs=[hbm] * 9,
            out_specs=hbm,
            scratch_shapes=[
                pltpu.VMEM((n_mem * QBLK, HS), jnp.bfloat16),
                pltpu.VMEM((2, WINDOW + group, HS), jnp.bfloat16),
                pltpu.VMEM((2, spare + 1, MBLK, HS), jnp.bfloat16),
                pltpu.VMEM((n_mem * QBLK, HS), jnp.float32),
                pltpu.VMEM((n_mem * QBLK, HS), jnp.bfloat16),
                pltpu.VMEM(lists.shape, jnp.int32),
                pltpu.VMEM(counts.shape, jnp.int32),
                pltpu.VMEM(lists.shape, jnp.int32),
                pltpu.SMEM(lists.shape, jnp.int32),
                pltpu.SMEM(docs.shape, jnp.int32),
                pltpu.SMEM(gate.shape, jnp.float32),
                dma((4,)), dma, dma, dma, dma, dma((n_mem,)), dma, dma,
                dma, dma((n_mem // 2,)), dma, dma((n_mem // 2,)), dma, dma, dma, dma,
            ],
            compiler_params=pltpu.CompilerParams(
                collective_id=0, has_side_effects=True, vmem_limit_bytes=56 * 1024 * 1024
            ),
            name="memorizing_attention",
        )(q, k, v, by_block(mk), by_block(mv), lists, counts, docs, gate)

    in_specs = (
        P(("seq", "mem"), None),
        P(("seq", "mem"), None),
        P(("seq", "mem"), None),
        P("mem", None),
        P("mem", None),
        P("seq", None),
        P("seq"),
        P(),
        P(),
    )
    return jax.shard_map(
        on_device, mesh=mesh, in_specs=in_specs, out_specs=P(("seq", "mem"), None), check_vma=False
    )
```

```python
import functools

import jax
import jax.numpy as jnp
from jax import lax
from jax.experimental import pallas as pl
from jax.experimental.pallas import tpu as pltpu
from jax.sharding import PartitionSpec as P

MESH = pl.DeviceIdType.MESH

WINDOW = 1024
QBLK = 64
MBLK = 64
LIST = 8
HS = 128
HEADS = 8
BATCH = 4
OWN = 4
MASKED = -1e30
LOG2E = 1.4426950408889634
COEF = float(HS) ** -0.5 * LOG2E


def aligned(first, size):
    return pl.ds(pl.multiple_of(first, size), size)


def arrived(ref, sem):
    pltpu.make_async_copy(ref, ref, sem).wait()


def kernel(
    n_seq, n_mem, tok, shard,
    q_ref, k_ref, v_ref, mk_ref, mv_ref, lists_ref, counts_ref, docs_ref, gate_ref,
    out_ref,
    qbuf, kvbuf, membuf, mixed, obuf, lists, counts, slots_vmem, slots, docs, gates,
    small_sem, slot_sem, q_send, kv_send, q_recv, kv_recv, halo_send, halo_recv,
    mem_send, mem_recv, z_send, z_recv, swap_send, swap_recv, out_send, out_recv,
):
    s = lax.axis_index("seq")
    m = lax.axis_index("mem")
    core = lax.rem(s, 2)
    z_half = lax.rem(s // 2, 2)
    head = m // 2
    parity = lax.rem(m, 2)
    has_prv, has_nxt = s > 0, s < n_seq - 1
    nxt = {"seq": s + 1, "mem": m}
    prv = {"seq": s - 1, "mem": m}
    along_z = {"seq": s + 2 - 4 * z_half, "mem": m}
    partner = {"seq": s + 1 - 2 * core, "mem": m}
    n_rank = n_mem // 2
    blocks = shard // MBLK
    swapped = blocks - OWN
    spare = n_rank * blocks
    group = n_mem * tok

    smalls = (
        pltpu.make_async_copy(lists_ref, lists, small_sem.at[0]),
        pltpu.make_async_copy(counts_ref, counts, small_sem.at[1]),
        pltpu.make_async_copy(docs_ref, docs, small_sem.at[2]),
        pltpu.make_async_copy(gate_ref, gates, small_sem.at[3]),
    )
    for copy in smalls:
        copy.start()

    barrier = pltpu.get_barrier_semaphore()

    def greet(i, c):
        t = lax.rem(m + 1 + i, n_mem)
        pl.semaphore_signal(barrier, inc=1, device_id={"seq": s, "mem": t}, device_id_type=MESH)
        return c

    lax.fori_loop(0, n_mem - 1, greet, 0)
    for there, other in ((has_nxt, nxt), (has_prv, prv), (s >= 0, along_z)):

        @pl.when(there)
        def _(other=other):
            pl.semaphore_signal(barrier, inc=1, device_id=other, device_id_type=MESH)

    def cols(h):
        return aligned(h * HS, HS)

    def q_src(t):
        first = QBLK * lax.rem(lax.rem(t, 2) + m, 2)
        return q_ref.at[aligned(first, QBLK), cols(t // 2)]

    def kv_src(ref, t):
        return ref.at[:, cols(t // 2)]

    def mem_src(ref, h):
        return ref.at[pl.ds(z_half * swapped, OWN), :, cols(h)]

    def fetched(r):
        return membuf.at[core, pl.ds(r * blocks + z_half * swapped, OWN)]

    def along(r, z):
        return membuf.at[core, pl.ds(r * blocks + z * OWN, swapped)]

    def kv_rows(src):
        return aligned(WINDOW + src * tok, tok)

    q_dst = qbuf.at[aligned(m * QBLK, QBLK)]
    mem_dst = fetched(head)
    for on_core, ref in ((0, mk_ref), (1, mv_ref)):

        @pl.when(core == on_core)
        def _(ref=ref):
            pltpu.make_async_copy(mem_src(ref, head), mem_dst, mem_recv.at[head]).start()

    pltpu.make_async_copy(q_src(m), q_dst, q_recv).start()
    for kind, ref in enumerate((k_ref, v_ref)):
        pltpu.make_async_copy(kv_src(ref, m), kvbuf.at[kind, kv_rows(m)], kv_recv.at[m]).start()

    membuf[:, spare] = jnp.zeros((2, MBLK, HS), jnp.bfloat16)

    @pl.when(jnp.logical_not(has_prv))
    def _():
        kvbuf[:, :WINDOW] = jnp.zeros((2, WINDOW, HS), jnp.bfloat16)

    inner = has_prv & has_nxt

    @pl.when(inner)
    def _():
        pl.semaphore_wait(barrier, n_mem + 2)

    @pl.when(jnp.logical_not(inner))
    def _():
        pl.semaphore_wait(barrier, n_mem + 1)

    for on_core, ref in ((0, mk_ref), (1, mv_ref)):

        @pl.when(core == on_core)
        def _(ref=ref):
            def body(i, c):
                h = lax.rem(head + 1 + i, HEADS)
                to = {"seq": s, "mem": 2 * h + parity}
                pltpu.make_async_remote_copy(
                    mem_src(ref, h), mem_dst, mem_send, mem_recv.at[head], to, MESH
                ).start()
                return c

            lax.fori_loop(0, HEADS - 1, body, 0)

    def send_q(i, c):
        t = lax.rem(m + 1 + i, n_mem)
        to = {"seq": s, "mem": t}
        pltpu.make_async_remote_copy(q_src(t), q_dst, q_send, q_recv, to, MESH).start()
        return c

    lax.fori_loop(0, n_mem - 1, send_q, 0)

    def send_kv(i, c):
        t = lax.rem(m + 1 + i, n_mem)
        to = {"seq": s, "mem": t}
        for kind, ref in enumerate((k_ref, v_ref)):
            pltpu.make_async_remote_copy(
                kv_src(ref, t), kvbuf.at[kind, kv_rows(m)], kv_send, kv_recv.at[m], to, MESH
            ).start()
        return c


    for copy in smalls:
        copy.wait()
    named = [lists[j : j + 1, :] for j in range(LIST)]
    for j in range(LIST):
        ok = j < counts[...]
        for e in range(j):
            ok = ok & (named[e] != named[j])
        place = lax.shift_right_logical(named[j], 4) * blocks + (named[j] & (blocks - 1))
        slots_vmem[j : j + 1, :] = jnp.where(ok, place, spare)
    to_slots = pltpu.make_async_copy(slots_vmem, slots, slot_sem)
    to_slots.start()

    def pass_first(i, c):
        r = lax.rem(head + n_rank - i, n_rank)
        got, gives = fetched(r), along(r, z_half)
        arrived(got, mem_recv.at[r])
        pltpu.make_async_remote_copy(gives, gives, z_send, z_recv.at[r], along_z, MESH).start()
        pltpu.make_async_remote_copy(got, got, swap_send, swap_recv, partner, MESH).start()
        return c

    lax.fori_loop(0, n_rank, pass_first, 0)
    lax.fori_loop(0, n_mem - 1, send_kv, 0)

    def pass_second(i, c):
        r = lax.rem(head + n_rank - i, n_rank)
        got = along(r, 1 - z_half)
        arrived(got, z_recv.at[r])
        pltpu.make_async_remote_copy(got, got, swap_send, swap_recv, partner, MESH).start()
        return c

    lax.fori_loop(0, n_rank, pass_second, 0)

    gate = 1.0 / (1.0 + jnp.exp(-jnp.full((1, HS), gates[head], jnp.float32)))
    lane_slot = lax.broadcasted_iota(jnp.int32, (1, LIST * MBLK), 1) // MBLK

    def half_of(b):
        return lax.rem(parity + b, 2)

    def softmax(sc):
        w = jnp.exp2((sc - jnp.max(sc, axis=1, keepdims=True)) * COEF)
        return w.astype(jnp.bfloat16), jnp.sum(w, axis=1, keepdims=True)

    def scores(q, k):
        return lax.dot_general(q, k, (((1,), (1,)), ((), ())), preferred_element_type=jnp.float32)

    def mem_pair(i, c):
        keys, values, places = [], [], []
        for b in (2 * i, 2 * i + 1):
            row = 2 * b + half_of(b)
            ids = [slots[j, row] for j in range(LIST)]
            place = jnp.zeros((1, LIST * MBLK), jnp.int32)
            for j in range(LIST):
                place = jnp.where(lane_slot == j, ids[j], place)
            keys.append(jnp.concatenate([membuf[0, x] for x in ids], axis=0))
            values.append(jnp.concatenate([membuf[1, x] for x in ids], axis=0))
            places.append(jnp.broadcast_to(place, (QBLK, LIST * MBLK)))
        rows = aligned(2 * i * QBLK, 2 * QBLK)
        q = qbuf[rows, :]
        none = jnp.zeros((QBLK, HS), jnp.bfloat16)
        q = jnp.concatenate(
            [jnp.concatenate([q[:QBLK], none], axis=1), jnp.concatenate([none, q[QBLK:]], axis=1)], axis=0
        )
        sc = scores(q, jnp.concatenate(keys, axis=1))
        w, total = softmax(jnp.where(jnp.concatenate(places, axis=0) < spare, sc, MASKED))
        both = jnp.dot(w, jnp.concatenate(values, axis=1), preferred_element_type=jnp.float32)
        read = jnp.concatenate([both[:QBLK, :HS], both[QBLK:, HS:]], axis=0)
        mixed[rows, :] = gate * (read / total)
        return c

    reach = WINDOW // tok

    late = n_mem - reach

    def take(src):
        arrived(kvbuf.at[:, kv_rows(src)], kv_recv.at[src])

    def pass_halo(i, c):
        place = lax.rem(m + n_mem - i, reach)
        src = late + place
        take(src)

        @pl.when(has_nxt)
        def _():
            dst = kvbuf.at[:, aligned(place * tok, tok)]
            pltpu.make_async_remote_copy(
                kvbuf.at[:, kv_rows(src)], dst, halo_send, halo_recv, nxt, MESH
            ).start()

        return c

    to_slots.wait()
    arrived(qbuf, q_recv)
    arrived(membuf.at[1 - core, pl.ds(0, spare)], swap_recv)
    lax.fori_loop(0, n_mem // 2, mem_pair, 0, unroll=2)
    lax.fori_loop(0, reach, pass_halo, 0)

    def take_rest(src, c):
        take(src)
        return c

    lax.fori_loop(0, late, take_rest, 0)

    keys = WINDOW + BATCH * tok
    batches = n_mem // BATCH

    def local_batch(i, c):
        b = BATCH * i
        rows = aligned(b * QBLK, BATCH * QBLK)
        span = pl.ds(pl.multiple_of(b * tok, tok), keys)
        sc = scores(qbuf[rows, :], kvbuf[0, span, :])
        row = lax.broadcasted_iota(jnp.int32, (BATCH * QBLK, 1), 0)
        block = row // QBLK
        until = WINDOW + block * tok + QBLK * lax.rem(parity + block, 2) + lax.rem(row, QBLK)
        base = s * group + b * tok - WINDOW
        token = base + until
        first = jnp.zeros((BATCH * QBLK, 1), jnp.int32)
        for d in range(docs_ref.shape[0]):
            start = docs[d]
            first = jnp.maximum(first, jnp.where(start <= token, start, 0))
        low = jnp.maximum(first - base, until - (WINDOW - 1))
        col = lax.broadcasted_iota(jnp.int32, (BATCH * QBLK, keys), 1)
        sc = jnp.where(col >= low, sc, MASKED)
        tail = jnp.where(col[:, WINDOW:] <= until, sc[:, WINDOW:], MASKED)
        w, total = softmax(jnp.concatenate([sc[:, :WINDOW], tail], axis=1))
        local = jnp.dot(w, kvbuf[1, span, :], preferred_element_type=jnp.float32) / total
        obuf[rows, :] = (mixed[rows, :] + (1.0 - gate) * local).astype(jnp.bfloat16)
        for j in range(BATCH):
            t = b + j
            src = obuf.at[aligned(t * QBLK, QBLK)]
            dst = out_ref.at[aligned(QBLK * half_of(t), QBLK), cols(head)]

            @pl.when(t != m)
            def _():
                pltpu.make_async_remote_copy(
                    src, dst, out_send, out_recv, {"seq": s, "mem": t}, MESH
                ).start()

            @pl.when(t == m)
            def _():
                pltpu.make_async_copy(src, dst, out_recv).start()

        return c

    lax.fori_loop(batches // 2, batches, local_batch, 0)

    @pl.when(has_prv)
    def _():
        arrived(kvbuf.at[:, pl.ds(0, WINDOW)], halo_recv)

    lax.fori_loop(0, batches // 2, local_batch, 0)

    arrived(membuf.at[0, pl.ds(0, (HEADS - 1) * OWN)], mem_send)
    arrived(membuf.at[0, pl.ds(0, n_rank * swapped)], z_send)
    arrived(membuf.at[0, pl.ds(0, spare)], swap_send)
    arrived(qbuf.at[pl.ds(0, (n_mem - 1) * QBLK)], q_send)
    arrived(kvbuf.at[:, pl.ds(0, (n_mem - 1) * tok)], kv_send)

    @pl.when(has_nxt)
    def _():
        arrived(kvbuf.at[:, pl.ds(0, WINDOW)], halo_send)

    arrived(obuf.at[pl.ds(0, (n_mem - 1) * QBLK)], out_send)
    arrived(out_ref, out_recv)


def solution(mesh):
    n_seq, n_mem = mesh.shape["seq"], mesh.shape["mem"]

    def on_device(q, k, v, mk, mv, lists, counts, docs, gate):
        tok, width = q.shape
        shard = mk.shape[0]
        group = n_mem * tok
        spare = n_mem // 2 * shard // MBLK
        lists = lists.T
        counts = counts.reshape(1, -1)
        by_block = lambda x: x.reshape(shard // MBLK, MBLK, width)
        hbm = pl.BlockSpec(memory_space=pl.ANY)
        dma = pltpu.SemaphoreType.DMA
        return pl.pallas_call(
            functools.partial(kernel, n_seq, n_mem, tok, shard),
            out_shape=jax.ShapeDtypeStruct((tok, width), jnp.bfloat16),
            in_specs=[hbm] * 9,
            out_specs=hbm,
            scratch_shapes=[
                pltpu.VMEM((n_mem * QBLK, HS), jnp.bfloat16),
                pltpu.VMEM((2, WINDOW + group, HS), jnp.bfloat16),
                pltpu.VMEM((2, spare + 1, MBLK, HS), jnp.bfloat16),
                pltpu.VMEM((n_mem * QBLK, HS), jnp.float32),
                pltpu.VMEM((n_mem * QBLK, HS), jnp.bfloat16),
                pltpu.VMEM(lists.shape, jnp.int32),
                pltpu.VMEM(counts.shape, jnp.int32),
                pltpu.VMEM(lists.shape, jnp.int32),
                pltpu.SMEM(lists.shape, jnp.int32),
                pltpu.SMEM(docs.shape, jnp.int32),
                pltpu.SMEM(gate.shape, jnp.float32),
                dma((4,)), dma, dma, dma, dma, dma((n_mem,)), dma, dma,
                dma, dma((n_mem // 2,)), dma, dma((n_mem // 2,)), dma, dma, dma, dma,
            ],
            compiler_params=pltpu.CompilerParams(
                collective_id=0, has_side_effects=True, vmem_limit_bytes=56 * 1024 * 1024
            ),
            name="memorizing_attention",
        )(q, k, v, by_block(mk), by_block(mv), lists, counts, docs, gate)

    in_specs = (
        P(("seq", "mem"), None),
        P(("seq", "mem"), None),
        P(("seq", "mem"), None),
        P("mem", None),
        P("mem", None),
        P("seq", None),
        P("seq"),
        P(),
        P(),
    )
    return jax.shard_map(
        on_device, mesh=mesh, in_specs=in_specs, out_specs=P(("seq", "mem"), None), check_vma=False
    )
```

```python
import functools

import jax
import jax.numpy as jnp
from jax import lax
from jax.experimental import pallas as pl
from jax.experimental.pallas import tpu as pltpu
from jax.sharding import PartitionSpec as P

MESH = pl.DeviceIdType.MESH

WINDOW = 1024
QBLK = 64
MBLK = 64
LIST = 8
HS = 128
HEADS = 8
BATCH = 4
OWN = 4
MASKED = -1e30
LOG2E = 1.4426950408889634
COEF = float(HS) ** -0.5 * LOG2E


def aligned(first, size):
    return pl.ds(pl.multiple_of(first, size), size)


def arrived(ref, sem):
    pltpu.make_async_copy(ref, ref, sem).wait()


def kernel(
    n_seq, n_mem, tok, shard,
    q_ref, k_ref, v_ref, mk_ref, mv_ref, lists_ref, counts_ref, docs_ref, gate_ref,
    out_ref,
    qbuf, kvbuf, membuf, mixed, obuf, lists, counts, slots_vmem, slots, docs, gates,
    small_sem, slot_sem, q_send, kv_send, q_recv, kv_recv, halo_send, halo_recv,
    mem_send, mem_recv, z_send, z_recv, swap_send, swap_recv, out_send, out_recv,
):
    s = lax.axis_index("seq")
    m = lax.axis_index("mem")
    core = lax.rem(s, 2)
    z_half = lax.rem(s // 2, 2)
    head = m // 2
    parity = lax.rem(m, 2)
    has_prv, has_nxt = s > 0, s < n_seq - 1
    nxt = {"seq": s + 1, "mem": m}
    prv = {"seq": s - 1, "mem": m}
    along_z = {"seq": s + 2 - 4 * z_half, "mem": m}
    partner = {"seq": s + 1 - 2 * core, "mem": m}
    n_rank = n_mem // 2
    blocks = shard // MBLK
    swapped = blocks - OWN
    spare = n_rank * blocks
    group = n_mem * tok

    smalls = (
        pltpu.make_async_copy(lists_ref, lists, small_sem.at[0]),
        pltpu.make_async_copy(counts_ref, counts, small_sem.at[1]),
        pltpu.make_async_copy(docs_ref, docs, small_sem.at[2]),
        pltpu.make_async_copy(gate_ref, gates, small_sem.at[3]),
    )
    for copy in smalls:
        copy.start()

    barrier = pltpu.get_barrier_semaphore()

    def greet(i, c):
        t = lax.rem(m + 1 + i, n_mem)
        pl.semaphore_signal(barrier, inc=1, device_id={"seq": s, "mem": t}, device_id_type=MESH)
        return c

    lax.fori_loop(0, n_mem - 1, greet, 0)
    for there, other in ((has_nxt, nxt), (has_prv, prv), (s >= 0, along_z)):

        @pl.when(there)
        def _(other=other):
            pl.semaphore_signal(barrier, inc=1, device_id=other, device_id_type=MESH)

    def cols(h):
        return aligned(h * HS, HS)

    def q_src(t):
        first = QBLK * lax.rem(lax.rem(t, 2) + m, 2)
        return q_ref.at[aligned(first, QBLK), cols(t // 2)]

    def kv_src(ref, t):
        return ref.at[:, cols(t // 2)]

    def mem_src(ref, h):
        return ref.at[pl.ds(z_half * swapped, OWN), :, cols(h)]

    def fetched(r):
        return membuf.at[core, pl.ds(r * blocks + z_half * swapped, OWN)]

    def along(r, z):
        return membuf.at[core, pl.ds(r * blocks + z * OWN, swapped)]

    def kv_rows(src):
        return aligned(WINDOW + src * tok, tok)

    q_dst = qbuf.at[aligned(m * QBLK, QBLK)]
    mem_dst = fetched(head)
    for on_core, ref in ((0, mk_ref), (1, mv_ref)):

        @pl.when(core == on_core)
        def _(ref=ref):
            pltpu.make_async_copy(mem_src(ref, head), mem_dst, mem_recv.at[head]).start()

    pltpu.make_async_copy(q_src(m), q_dst, q_recv).start()
    for kind, ref in enumerate((k_ref, v_ref)):
        pltpu.make_async_copy(kv_src(ref, m), kvbuf.at[kind, kv_rows(m)], kv_recv.at[m]).start()

    membuf[:, spare] = jnp.zeros((2, MBLK, HS), jnp.bfloat16)

    @pl.when(jnp.logical_not(has_prv))
    def _():
        kvbuf[:, :WINDOW] = jnp.zeros((2, WINDOW, HS), jnp.bfloat16)

    inner = has_prv & has_nxt

    @pl.when(inner)
    def _():
        pl.semaphore_wait(barrier, n_mem + 2)

    @pl.when(jnp.logical_not(inner))
    def _():
        pl.semaphore_wait(barrier, n_mem + 1)

    for on_core, ref in ((0, mk_ref), (1, mv_ref)):

        @pl.when(core == on_core)
        def _(ref=ref):
            def body(i, c):
                h = lax.rem(head + 1 + i, HEADS)
                to = {"seq": s, "mem": 2 * h + parity}
                pltpu.make_async_remote_copy(
                    mem_src(ref, h), mem_dst, mem_send, mem_recv.at[head], to, MESH
                ).start()
                return c

            lax.fori_loop(0, HEADS - 1, body, 0)

    def send_q(i, c):
        t = lax.rem(m + 1 + i, n_mem)
        to = {"seq": s, "mem": t}
        pltpu.make_async_remote_copy(q_src(t), q_dst, q_send, q_recv, to, MESH).start()
        return c

    lax.fori_loop(0, n_mem - 1, send_q, 0)

    def send_kv(i, c):
        t = lax.rem(m + 1 + i, n_mem)
        to = {"seq": s, "mem": t}
        for kind, ref in enumerate((k_ref, v_ref)):
            pltpu.make_async_remote_copy(
                kv_src(ref, t), kvbuf.at[kind, kv_rows(m)], kv_send, kv_recv.at[m], to, MESH
            ).start()
        return c


    early = (m >= n_mem - WINDOW // tok) | (m == 0)

    @pl.when(early)
    def _():
        lax.fori_loop(0, n_mem - 1, send_kv, 0)

    for copy in smalls:
        copy.wait()
    named = [lists[j : j + 1, :] for j in range(LIST)]
    for j in range(LIST):
        ok = j < counts[...]
        for e in range(j):
            ok = ok & (named[e] != named[j])
        place = lax.shift_right_logical(named[j], 4) * blocks + (named[j] & (blocks - 1))
        slots_vmem[j : j + 1, :] = jnp.where(ok, place, spare)
    to_slots = pltpu.make_async_copy(slots_vmem, slots, slot_sem)
    to_slots.start()

    def pass_first(i, c):
        r = lax.rem(head + n_rank - i, n_rank)
        got, gives = fetched(r), along(r, z_half)
        arrived(got, mem_recv.at[r])
        pltpu.make_async_remote_copy(gives, gives, z_send, z_recv.at[r], along_z, MESH).start()
        pltpu.make_async_remote_copy(got, got, swap_send, swap_recv, partner, MESH).start()
        return c

    lax.fori_loop(0, n_rank, pass_first, 0)

    @pl.when(jnp.logical_not(early))
    def _():
        lax.fori_loop(0, n_mem - 1, send_kv, 0)


    def pass_second(i, c):
        r = lax.rem(head + n_rank - i, n_rank)
        got = along(r, 1 - z_half)
        arrived(got, z_recv.at[r])
        pltpu.make_async_remote_copy(got, got, swap_send, swap_recv, partner, MESH).start()
        return c

    lax.fori_loop(0, n_rank, pass_second, 0)

    gate = 1.0 / (1.0 + jnp.exp(-jnp.full((1, HS), gates[head], jnp.float32)))
    lane_slot = lax.broadcasted_iota(jnp.int32, (1, LIST * MBLK), 1) // MBLK

    def half_of(b):
        return lax.rem(parity + b, 2)

    def softmax(sc):
        w = jnp.exp2((sc - jnp.max(sc, axis=1, keepdims=True)) * COEF)
        return w.astype(jnp.bfloat16), jnp.sum(w, axis=1, keepdims=True)

    def scores(q, k):
        return lax.dot_general(q, k, (((1,), (1,)), ((), ())), preferred_element_type=jnp.float32)

    def mem_pair(i, c):
        keys, values, places = [], [], []
        for b in (2 * i, 2 * i + 1):
            row = 2 * b + half_of(b)
            ids = [slots[j, row] for j in range(LIST)]
            place = jnp.zeros((1, LIST * MBLK), jnp.int32)
            for j in range(LIST):
                place = jnp.where(lane_slot == j, ids[j], place)
            keys.append(jnp.concatenate([membuf[0, x] for x in ids], axis=0))
            values.append(jnp.concatenate([membuf[1, x] for x in ids], axis=0))
            places.append(jnp.broadcast_to(place, (QBLK, LIST * MBLK)))
        rows = aligned(2 * i * QBLK, 2 * QBLK)
        q = qbuf[rows, :]
        none = jnp.zeros((QBLK, HS), jnp.bfloat16)
        q = jnp.concatenate(
            [jnp.concatenate([q[:QBLK], none], axis=1), jnp.concatenate([none, q[QBLK:]], axis=1)], axis=0
        )
        sc = scores(q, jnp.concatenate(keys, axis=1))
        w, total = softmax(jnp.where(jnp.concatenate(places, axis=0) < spare, sc, MASKED))
        both = jnp.dot(w, jnp.concatenate(values, axis=1), preferred_element_type=jnp.float32)
        read = jnp.concatenate([both[:QBLK, :HS], both[QBLK:, HS:]], axis=0)
        mixed[rows, :] = gate * (read / total)
        return c

    reach = WINDOW // tok

    late = n_mem - reach

    def take(src):
        arrived(kvbuf.at[:, kv_rows(src)], kv_recv.at[src])

    def pass_halo(i, c):
        place = lax.rem(m + n_mem - i, reach)
        src = late + place
        take(src)

        @pl.when(has_nxt)
        def _():
            dst = kvbuf.at[:, aligned(place * tok, tok)]
            pltpu.make_async_remote_copy(
                kvbuf.at[:, kv_rows(src)], dst, halo_send, halo_recv, nxt, MESH
            ).start()

        return c

    to_slots.wait()
    arrived(qbuf, q_recv)
    arrived(membuf.at[1 - core, pl.ds(0, spare)], swap_recv)

    def halo_and_mem(i, c):
        pass_halo(i, c)
        mem_pair(i, c)
        return c

    lax.fori_loop(0, reach, halo_and_mem, 0)

    def take_rest(src, c):
        take(src)
        return c

    lax.fori_loop(0, late, take_rest, 0)

    keys = WINDOW + BATCH * tok
    batches = n_mem // BATCH

    def local_batch(i, c):
        b = BATCH * i
        rows = aligned(b * QBLK, BATCH * QBLK)
        span = pl.ds(pl.multiple_of(b * tok, tok), keys)
        sc = scores(qbuf[rows, :], kvbuf[0, span, :])
        row = lax.broadcasted_iota(jnp.int32, (BATCH * QBLK, 1), 0)
        block = row // QBLK
        until = WINDOW + block * tok + QBLK * lax.rem(parity + block, 2) + lax.rem(row, QBLK)
        base = s * group + b * tok - WINDOW
        token = base + until
        first = jnp.zeros((BATCH * QBLK, 1), jnp.int32)
        for d in range(docs_ref.shape[0]):
            start = docs[d]
            first = jnp.maximum(first, jnp.where(start <= token, start, 0))
        low = jnp.maximum(first - base, until - (WINDOW - 1))
        col = lax.broadcasted_iota(jnp.int32, (BATCH * QBLK, keys), 1)
        sc = jnp.where(col >= low, sc, MASKED)
        tail = jnp.where(col[:, WINDOW:] <= until, sc[:, WINDOW:], MASKED)
        w, total = softmax(jnp.concatenate([sc[:, :WINDOW], tail], axis=1))
        local = jnp.dot(w, kvbuf[1, span, :], preferred_element_type=jnp.float32) / total
        obuf[rows, :] = (mixed[rows, :] + (1.0 - gate) * local).astype(jnp.bfloat16)
        for j in range(BATCH):
            t = b + j
            src = obuf.at[aligned(t * QBLK, QBLK)]
            dst = out_ref.at[aligned(QBLK * half_of(t), QBLK), cols(head)]

            @pl.when(t != m)
            def _():
                pltpu.make_async_remote_copy(
                    src, dst, out_send, out_recv, {"seq": s, "mem": t}, MESH
                ).start()

            @pl.when(t == m)
            def _():
                pltpu.make_async_copy(src, dst, out_recv).start()

        return c

    lax.fori_loop(batches // 2, batches, local_batch, 0)

    @pl.when(has_prv)
    def _():
        arrived(kvbuf.at[:, pl.ds(0, WINDOW)], halo_recv)

    lax.fori_loop(0, batches // 2, local_batch, 0)

    arrived(membuf.at[0, pl.ds(0, (HEADS - 1) * OWN)], mem_send)
    arrived(membuf.at[0, pl.ds(0, n_rank * swapped)], z_send)
    arrived(membuf.at[0, pl.ds(0, spare)], swap_send)
    arrived(qbuf.at[pl.ds(0, (n_mem - 1) * QBLK)], q_send)
    arrived(kvbuf.at[:, pl.ds(0, (n_mem - 1) * tok)], kv_send)

    @pl.when(has_nxt)
    def _():
        arrived(kvbuf.at[:, pl.ds(0, WINDOW)], halo_send)

    arrived(obuf.at[pl.ds(0, (n_mem - 1) * QBLK)], out_send)
    arrived(out_ref, out_recv)


def solution(mesh):
    n_seq, n_mem = mesh.shape["seq"], mesh.shape["mem"]

    def on_device(q, k, v, mk, mv, lists, counts, docs, gate):
        tok, width = q.shape
        shard = mk.shape[0]
        group = n_mem * tok
        spare = n_mem // 2 * shard // MBLK
        lists = lists.T
        counts = counts.reshape(1, -1)
        by_block = lambda x: x.reshape(shard // MBLK, MBLK, width)
        hbm = pl.BlockSpec(memory_space=pl.ANY)
        dma = pltpu.SemaphoreType.DMA
        return pl.pallas_call(
            functools.partial(kernel, n_seq, n_mem, tok, shard),
            out_shape=jax.ShapeDtypeStruct((tok, width), jnp.bfloat16),
            in_specs=[hbm] * 9,
            out_specs=hbm,
            scratch_shapes=[
                pltpu.VMEM((n_mem * QBLK, HS), jnp.bfloat16),
                pltpu.VMEM((2, WINDOW + group, HS), jnp.bfloat16),
                pltpu.VMEM((2, spare + 1, MBLK, HS), jnp.bfloat16),
                pltpu.VMEM((n_mem * QBLK, HS), jnp.float32),
                pltpu.VMEM((n_mem * QBLK, HS), jnp.bfloat16),
                pltpu.VMEM(lists.shape, jnp.int32),
                pltpu.VMEM(counts.shape, jnp.int32),
                pltpu.VMEM(lists.shape, jnp.int32),
                pltpu.SMEM(lists.shape, jnp.int32),
                pltpu.SMEM(docs.shape, jnp.int32),
                pltpu.SMEM(gate.shape, jnp.float32),
                dma((4,)), dma, dma, dma, dma, dma((n_mem,)), dma, dma,
                dma, dma((n_mem // 2,)), dma, dma((n_mem // 2,)), dma, dma, dma, dma,
            ],
            compiler_params=pltpu.CompilerParams(
                collective_id=0, has_side_effects=True, vmem_limit_bytes=107 * 512 * 1024
            ),
            name="memorizing_attention",
        )(q, k, v, by_block(mk), by_block(mv), lists, counts, docs, gate)

    in_specs = (
        P(("seq", "mem"), None),
        P(("seq", "mem"), None),
        P(("seq", "mem"), None),
        P("mem", None),
        P("mem", None),
        P("seq", None),
        P("seq"),
        P(),
        P(),
    )
    return jax.shard_map(
        on_device, mesh=mesh, in_specs=in_specs, out_specs=P(("seq", "mem"), None), check_vma=False
    )
```

```python
import functools

import jax
import jax.numpy as jnp
from jax import lax
from jax.experimental import pallas as pl
from jax.experimental.pallas import tpu as pltpu
from jax.sharding import PartitionSpec as P

MESH = pl.DeviceIdType.MESH

WINDOW = 1024
QBLK = 64
MBLK = 64
LIST = 8
HS = 128
HEADS = 8
BATCH = 4
OWN = 4
MASKED = -1e30
LOG2E = 1.4426950408889634
COEF = float(HS) ** -0.5 * LOG2E


def aligned(first, size):
    return pl.ds(pl.multiple_of(first, size), size)


def arrived(ref, sem):
    pltpu.make_async_copy(ref, ref, sem).wait()


def kernel(
    n_seq, n_mem, tok, shard,
    q_ref, k_ref, v_ref, mk_ref, mv_ref, lists_ref, counts_ref, docs_ref, gate_ref,
    out_ref,
    qbuf, kvbuf, membuf, mixed, obuf, lists, counts, slots_vmem, slots, docs, gates,
    small_sem, slot_sem, q_send, kv_send, q_recv, kv_recv, halo_send, halo_recv,
    mem_send, mem_recv, z_send, z_recv, swap_send, swap_recv, out_send, out_recv,
):
    s = lax.axis_index("seq")
    m = lax.axis_index("mem")
    core = lax.rem(s, 2)
    z_half = lax.rem(s // 2, 2)
    head = m // 2
    parity = lax.rem(m, 2)
    has_prv, has_nxt = s > 0, s < n_seq - 1
    nxt = {"seq": s + 1, "mem": m}
    prv = {"seq": s - 1, "mem": m}
    along_z = {"seq": s + 2 - 4 * z_half, "mem": m}
    partner = {"seq": s + 1 - 2 * core, "mem": m}
    n_rank = n_mem // 2
    blocks = shard // MBLK
    swapped = blocks - OWN
    spare = n_rank * blocks
    group = n_mem * tok

    smalls = (
        pltpu.make_async_copy(lists_ref, lists, small_sem.at[0]),
        pltpu.make_async_copy(counts_ref, counts, small_sem.at[1]),
        pltpu.make_async_copy(docs_ref, docs, small_sem.at[2]),
        pltpu.make_async_copy(gate_ref, gates, small_sem.at[3]),
    )
    for copy in smalls:
        copy.start()

    barrier = pltpu.get_barrier_semaphore()

    def greet(i, c):
        t = lax.rem(m + 1 + i, n_mem)
        pl.semaphore_signal(barrier, inc=1, device_id={"seq": s, "mem": t}, device_id_type=MESH)
        return c

    lax.fori_loop(0, n_mem - 1, greet, 0)
    for there, other in ((has_nxt, nxt), (has_prv, prv), (s >= 0, along_z)):

        @pl.when(there)
        def _(other=other):
            pl.semaphore_signal(barrier, inc=1, device_id=other, device_id_type=MESH)

    def cols(h):
        return aligned(h * HS, HS)

    def q_src(t):
        first = QBLK * lax.rem(lax.rem(t, 2) + m, 2)
        return q_ref.at[aligned(first, QBLK), cols(t // 2)]

    def kv_src(ref, t):
        return ref.at[:, cols(t // 2)]

    def mem_src(ref, h):
        return ref.at[pl.ds(z_half * swapped, OWN), :, cols(h)]

    def fetched(r):
        return membuf.at[core, pl.ds(r * blocks + z_half * swapped, OWN)]

    def along(r, z):
        return membuf.at[core, pl.ds(r * blocks + z * OWN, swapped)]

    def kv_rows(src):
        return aligned(WINDOW + src * tok, tok)

    q_dst = qbuf.at[aligned(m * QBLK, QBLK)]
    mem_dst = fetched(head)
    for on_core, ref in ((0, mk_ref), (1, mv_ref)):

        @pl.when(core == on_core)
        def _(ref=ref):
            pltpu.make_async_copy(mem_src(ref, head), mem_dst, mem_recv.at[head]).start()

    pltpu.make_async_copy(q_src(m), q_dst, q_recv).start()
    for kind, ref in enumerate((k_ref, v_ref)):
        pltpu.make_async_copy(kv_src(ref, m), kvbuf.at[kind, kv_rows(m)], kv_recv.at[m]).start()

    membuf[:, spare] = jnp.zeros((2, MBLK, HS), jnp.bfloat16)

    @pl.when(jnp.logical_not(has_prv))
    def _():
        kvbuf[:, :WINDOW] = jnp.zeros((2, WINDOW, HS), jnp.bfloat16)

    inner = has_prv & has_nxt

    @pl.when(inner)
    def _():
        pl.semaphore_wait(barrier, n_mem + 2)

    @pl.when(jnp.logical_not(inner))
    def _():
        pl.semaphore_wait(barrier, n_mem + 1)

    for on_core, ref in ((0, mk_ref), (1, mv_ref)):

        @pl.when(core == on_core)
        def _(ref=ref):
            def body(i, c):
                h = lax.rem(head + 1 + i, HEADS)
                to = {"seq": s, "mem": 2 * h + parity}
                pltpu.make_async_remote_copy(
                    mem_src(ref, h), mem_dst, mem_send, mem_recv.at[head], to, MESH
                ).start()
                return c

            lax.fori_loop(0, HEADS - 1, body, 0)

    def send_q(i, c):
        t = lax.rem(m + 1 + i, n_mem)
        to = {"seq": s, "mem": t}
        pltpu.make_async_remote_copy(q_src(t), q_dst, q_send, q_recv, to, MESH).start()
        return c

    lax.fori_loop(0, n_mem - 1, send_q, 0)

    def send_kv(i, c):
        t = lax.rem(m + 1 + i, n_mem)
        to = {"seq": s, "mem": t}
        for kind, ref in enumerate((k_ref, v_ref)):
            pltpu.make_async_remote_copy(
                kv_src(ref, t), kvbuf.at[kind, kv_rows(m)], kv_send, kv_recv.at[m], to, MESH
            ).start()
        return c


    early = (m >= n_mem - WINDOW // tok) | (m == 0)

    @pl.when(early)
    def _():
        lax.fori_loop(0, n_mem - 1, send_kv, 0)

    for copy in smalls:
        copy.wait()
    named = [lists[j : j + 1, :] for j in range(LIST)]
    for j in range(LIST):
        ok = j < counts[...]
        for e in range(j):
            ok = ok & (named[e] != named[j])
        place = lax.shift_right_logical(named[j], 4) * blocks + (named[j] & (blocks - 1))
        slots_vmem[j : j + 1, :] = jnp.where(ok, place, spare)
    to_slots = pltpu.make_async_copy(slots_vmem, slots, slot_sem)
    to_slots.start()

    def pass_first(i, c):
        r = lax.rem(head + n_rank - i, n_rank)
        got, gives = fetched(r), along(r, z_half)
        arrived(got, mem_recv.at[r])
        pltpu.make_async_remote_copy(gives, gives, z_send, z_recv.at[r], along_z, MESH).start()
        pltpu.make_async_remote_copy(got, got, swap_send, swap_recv, partner, MESH).start()
        return c

    lax.fori_loop(0, n_rank, pass_first, 0)

    @pl.when(jnp.logical_not(early))
    def _():
        lax.fori_loop(0, n_mem - 1, send_kv, 0)


    def pass_second(i, c):
        r = lax.rem(head + n_rank - i, n_rank)
        got = along(r, 1 - z_half)
        arrived(got, z_recv.at[r])
        pltpu.make_async_remote_copy(got, got, swap_send, swap_recv, partner, MESH).start()
        return c

    lax.fori_loop(0, n_rank, pass_second, 0)

    gate = 1.0 / (1.0 + jnp.exp(-jnp.full((1, HS), gates[head], jnp.float32)))
    lane_slot = lax.broadcasted_iota(jnp.int32, (1, LIST * MBLK), 1) // MBLK

    def half_of(b):
        return lax.rem(parity + b, 2)

    def softmax(sc):
        w = jnp.exp2((sc - jnp.max(sc, axis=1, keepdims=True)) * COEF)
        return w.astype(jnp.bfloat16), jnp.sum(w, axis=1, keepdims=True)

    def scores(q, k):
        return lax.dot_general(q, k, (((1,), (1,)), ((), ())), preferred_element_type=jnp.float32)

    def mem_pair(i, c):
        keys, values, places = [], [], []
        for b in (2 * i, 2 * i + 1):
            row = 2 * b + half_of(b)
            ids = [slots[j, row] for j in range(LIST)]
            place = jnp.zeros((1, LIST * MBLK), jnp.int32)
            for j in range(LIST):
                place = jnp.where(lane_slot == j, ids[j], place)
            keys.append(jnp.concatenate([membuf[0, x] for x in ids], axis=0))
            values.append(jnp.concatenate([membuf[1, x] for x in ids], axis=0))
            places.append(jnp.broadcast_to(place, (QBLK, LIST * MBLK)))
        rows = aligned(2 * i * QBLK, 2 * QBLK)
        q = qbuf[rows, :]
        none = jnp.zeros((QBLK, HS), jnp.bfloat16)
        q = jnp.concatenate(
            [jnp.concatenate([q[:QBLK], none], axis=1), jnp.concatenate([none, q[QBLK:]], axis=1)], axis=0
        )
        sc = scores(q, jnp.concatenate(keys, axis=1))
        w, total = softmax(jnp.where(jnp.concatenate(places, axis=0) < spare, sc, MASKED))
        both = jnp.dot(w, jnp.concatenate(values, axis=1), preferred_element_type=jnp.float32)
        read = jnp.concatenate([both[:QBLK, :HS], both[QBLK:, HS:]], axis=0)
        mixed[rows, :] = gate * (read / total)
        return c

    reach = WINDOW // tok

    late = n_mem - reach

    def take(src):
        arrived(kvbuf.at[:, kv_rows(src)], kv_recv.at[src])

    def pass_halo(i, c):
        place = lax.rem(m + n_mem - i, reach)
        src = late + place
        take(src)

        @pl.when(has_nxt)
        def _():
            dst = kvbuf.at[:, aligned(place * tok, tok)]
            pltpu.make_async_remote_copy(
                kvbuf.at[:, kv_rows(src)], dst, halo_send, halo_recv, nxt, MESH
            ).start()

        return c

    to_slots.wait()
    arrived(qbuf, q_recv)
    arrived(membuf.at[1 - core, pl.ds(0, spare)], swap_recv)

    def halo_and_mem(i, c):
        pass_halo(2 * i, c)
        pass_halo(2 * i + 1, c)
        mem_pair(2 * i, c)
        mem_pair(2 * i + 1, c)
        return c

    lax.fori_loop(0, reach // 2, halo_and_mem, 0)

    def take_rest(src, c):
        take(src)
        return c

    lax.fori_loop(0, late, take_rest, 0)

    keys = WINDOW + BATCH * tok
    batches = n_mem // BATCH

    def local_batch(i, c):
        b = BATCH * i
        rows = aligned(b * QBLK, BATCH * QBLK)
        span = pl.ds(pl.multiple_of(b * tok, tok), keys)
        sc = scores(qbuf[rows, :], kvbuf[0, span, :])
        row = lax.broadcasted_iota(jnp.int32, (BATCH * QBLK, 1), 0)
        block = row // QBLK
        until = WINDOW + block * tok + QBLK * lax.rem(parity + block, 2) + lax.rem(row, QBLK)
        base = s * group + b * tok - WINDOW
        token = base + until
        first = jnp.zeros((BATCH * QBLK, 1), jnp.int32)
        for d in range(docs_ref.shape[0]):
            start = docs[d]
            first = jnp.maximum(first, jnp.where(start <= token, start, 0))
        low = jnp.maximum(first - base, until - (WINDOW - 1))
        col = lax.broadcasted_iota(jnp.int32, (BATCH * QBLK, keys), 1)
        sc = jnp.where(col >= low, sc, MASKED)
        tail = jnp.where(col[:, WINDOW:] <= until, sc[:, WINDOW:], MASKED)
        w, total = softmax(jnp.concatenate([sc[:, :WINDOW], tail], axis=1))
        local = jnp.dot(w, kvbuf[1, span, :], preferred_element_type=jnp.float32) / total
        obuf[rows, :] = (mixed[rows, :] + (1.0 - gate) * local).astype(jnp.bfloat16)
        for j in range(BATCH):
            t = b + j
            src = obuf.at[aligned(t * QBLK, QBLK)]
            dst = out_ref.at[aligned(QBLK * half_of(t), QBLK), cols(head)]

            @pl.when(t != m)
            def _():
                pltpu.make_async_remote_copy(
                    src, dst, out_send, out_recv, {"seq": s, "mem": t}, MESH
                ).start()

            @pl.when(t == m)
            def _():
                pltpu.make_async_copy(src, dst, out_recv).start()

        return c

    lax.fori_loop(batches // 2, batches, local_batch, 0)

    @pl.when(has_prv)
    def _():
        arrived(kvbuf.at[:, pl.ds(0, WINDOW)], halo_recv)

    lax.fori_loop(0, batches // 2, local_batch, 0)

    arrived(membuf.at[0, pl.ds(0, (HEADS - 1) * OWN)], mem_send)
    arrived(membuf.at[0, pl.ds(0, n_rank * swapped)], z_send)
    arrived(membuf.at[0, pl.ds(0, spare)], swap_send)
    arrived(qbuf.at[pl.ds(0, (n_mem - 1) * QBLK)], q_send)
    arrived(kvbuf.at[:, pl.ds(0, (n_mem - 1) * tok)], kv_send)

    @pl.when(has_nxt)
    def _():
        arrived(kvbuf.at[:, pl.ds(0, WINDOW)], halo_send)

    arrived(obuf.at[pl.ds(0, (n_mem - 1) * QBLK)], out_send)
    arrived(out_ref, out_recv)


def solution(mesh):
    n_seq, n_mem = mesh.shape["seq"], mesh.shape["mem"]

    def on_device(q, k, v, mk, mv, lists, counts, docs, gate):
        tok, width = q.shape
        shard = mk.shape[0]
        group = n_mem * tok
        spare = n_mem // 2 * shard // MBLK
        lists = lists.T
        counts = counts.reshape(1, -1)
        by_block = lambda x: x.reshape(shard // MBLK, MBLK, width)
        hbm = pl.BlockSpec(memory_space=pl.ANY)
        dma = pltpu.SemaphoreType.DMA
        return pl.pallas_call(
            functools.partial(kernel, n_seq, n_mem, tok, shard),
            out_shape=jax.ShapeDtypeStruct((tok, width), jnp.bfloat16),
            in_specs=[hbm] * 9,
            out_specs=hbm,
            scratch_shapes=[
                pltpu.VMEM((n_mem * QBLK, HS), jnp.bfloat16),
                pltpu.VMEM((2, WINDOW + group, HS), jnp.bfloat16),
                pltpu.VMEM((2, spare + 1, MBLK, HS), jnp.bfloat16),
                pltpu.VMEM((n_mem * QBLK, HS), jnp.float32),
                pltpu.VMEM((n_mem * QBLK, HS), jnp.bfloat16),
                pltpu.VMEM(lists.shape, jnp.int32),
                pltpu.VMEM(counts.shape, jnp.int32),
                pltpu.VMEM(lists.shape, jnp.int32),
                pltpu.SMEM(lists.shape, jnp.int32),
                pltpu.SMEM(docs.shape, jnp.int32),
                pltpu.SMEM(gate.shape, jnp.float32),
                dma((4,)), dma, dma, dma, dma, dma((n_mem,)), dma, dma,
                dma, dma((n_mem // 2,)), dma, dma((n_mem // 2,)), dma, dma, dma, dma,
            ],
            compiler_params=pltpu.CompilerParams(
                collective_id=0, has_side_effects=True, vmem_limit_bytes=107 * 512 * 1024
            ),
            name="memorizing_attention",
        )(q, k, v, by_block(mk), by_block(mv), lists, counts, docs, gate)

    in_specs = (
        P(("seq", "mem"), None),
        P(("seq", "mem"), None),
        P(("seq", "mem"), None),
        P("mem", None),
        P("mem", None),
        P("seq", None),
        P("seq"),
        P(),
        P(),
    )
    return jax.shard_map(
        on_device, mesh=mesh, in_specs=in_specs, out_specs=P(("seq", "mem"), None), check_vma=False
    )
```
